256 devices in a mesh: head: 4 (over y_hi, core), blk: 64 (over x, z, y_lo).
Axes of the slice: x: 4, y: 4 (y_hi: 2, y_lo: 2; y = y_hi * 2 + y_lo), z: 8, core: 2. Of those that a mesh axis runs over, the one named last changes fastest.
Arguments:
- queries: bfloat16 [16384, 512], P(('blk', 'head')), may hold values from -6 to 6
- keys: bfloat16 [16384, 512], P(('blk', 'head')), may hold values from -6 to 6
- values: bfloat16 [16384, 512], P(('blk', 'head')), may hold values from -6 to 6
- upstream: bfloat16 [16384, 512], P(('blk', 'head')), may hold values from -6 to 6
Outputs:
- attended: bfloat16 [16384, 512], P(('blk', 'head'))
- query_grad: bfloat16 [16384, 512], P(('blk', 'head'))
- key_grad: bfloat16 [16384, 512], P(('blk', 'head'))
- value_grad: bfloat16 [16384, 512], P(('blk', 'head'))
The draws below stay inside these ranges and needn't reach their ends.
All inputs are finite; a program needn't handle non-finite values.
Results may differ from the reference program's by a relative error of at most 0.02.
Values may be sent and summed in bfloat16 or wider, within the bound.
No kernel may reach another device: no remote copies, remote signals or barrier semaphores. Data moves between devices by JAX's collectives and lax.ppermute only.
A program may use at most 64 MiB of HBM per device.

```python
import math
import jax
import jax.numpy as jnp
from jax import lax

DH = 128
HEADS = 4
HW = 512
SEQ = 16384


def draw_queries(key, part):
    key = jax.random.fold_in(key, 1)
    sample = jnp.clip(jax.random.normal(key, (SEQ, HW), jnp.float32) * 1.6, -6.0, 6.0)
    return sample.astype(jnp.bfloat16)


def draw_keys(key, part):
    key = jax.random.fold_in(key, 2)
    sample = jnp.clip(jax.random.normal(key, (SEQ, HW), jnp.float32) * 1.6, -6.0, 6.0)
    return sample.astype(jnp.bfloat16)


def block_scale(rng, extent, split, low, largest):
    def one(dim, blocks):
        draws = jax.random.uniform(jax.random.fold_in(jax.random.fold_in(rng, 6), dim), (blocks,), jnp.float32, low / len(split), largest / len(split))
        return jnp.repeat(jnp.exp(draws), extent[dim] // blocks).reshape((-1,) + (1,) * (len(extent) - dim - 1))

    factor_of = one(*split[0])
    for cut in split[1:]:
        factor_of = factor_of * one(*cut)
    return factor_of


def noise(own_key, shape, scale, limit, pieces=(), dtype=jnp.bfloat16):
    result = jax.random.normal(own_key, shape, jnp.float32) * scale
    if len(pieces) > 0:
        result = block_scale(own_key, shape, pieces, -0.22, 0.18) * result
    return jnp.clip(result, min=-limit, max=limit).astype(dtype)


def setup_inputs(seed: int = 0) -> dict:
    streams_of = jax.random.split(jax.random.key(seed), 5)
    return {
        "queries": draw_queries(jax.random.fold_in(streams_of[4], 71), 0),
        "keys": draw_keys(jax.random.fold_in(streams_of[4], 71), 0),
        "values": noise(streams_of[2], (SEQ, HW), 1.0, 6.0, ((0, 256),)),
        "upstream": noise(streams_of[3], (SEQ, HW), 1.0, 6.0, ((0, 256),)),
    }


def reference(queries, keys, values, upstream):
    scaling = 1.0 / math.sqrt(DH)

    def by_heads(matrix):
        return matrix.reshape(SEQ, HEADS, DH).transpose(1, 0, 2)

    def from_heads(stacked):
        return stacked.transpose(1, 0, 2).reshape(SEQ, HW)

    def one_head(operands):
        query_head, key_head, value_head, upstream_head = operands
        scores = jnp.dot(query_head, key_head.T, preferred_element_type=jnp.float32) * scaling
        row_max = lax.optimization_barrier(jnp.max(scores, axis=1, keepdims=True))
        log_total = row_max + jnp.log(lax.optimization_barrier(jnp.sum(jnp.exp(scores - row_max), axis=1, keepdims=True)))
        weights = jnp.exp(scores - log_total)
        weights_low = weights.astype(jnp.bfloat16)
        attended = jnp.dot(weights_low, value_head, preferred_element_type=jnp.float32).astype(jnp.bfloat16)
        delta = lax.optimization_barrier(jnp.sum(upstream_head.astype(jnp.float32) * attended.astype(jnp.float32), axis=1, keepdims=True))
        upstream_dot = jnp.dot(upstream_head, value_head.T, preferred_element_type=jnp.float32)
        score_grad = (weights * (upstream_dot - delta)).astype(jnp.bfloat16)
        query_grad = (jnp.dot(score_grad, key_head, preferred_element_type=jnp.float32) * scaling).astype(jnp.bfloat16)
        key_grad = (jnp.dot(score_grad.T, query_head, preferred_element_type=jnp.float32) * scaling).astype(jnp.bfloat16)
        value_grad = jnp.dot(weights_low.T, upstream_head, preferred_element_type=jnp.float32).astype(jnp.bfloat16)
        return (attended, query_grad, key_grad, value_grad)
    results = lax.map(one_head, (by_heads(queries), by_heads(keys), by_heads(values), by_heads(upstream)))
    return (from_heads(results[0]), from_heads(results[1]), from_heads(results[2]), from_heads(results[3]))
```

```python
import functools
import math

import jax
import jax.numpy as jnp
from jax import lax
from jax.experimental import pallas as pl
from jax.experimental.pallas import tpu as pltpu
from jax.sharding import Mesh, PartitionSpec as P

DH = 128
HALF = 256
SCALING = 1.0 / math.sqrt(DH)
SCALING2 = SCALING * math.log2(math.e)
F32 = jnp.float32
BF16 = jnp.bfloat16
LINE = ("z",)
PLANE = ("yh", "x", "yl")
TOKENS = P(("x", "z", "yl", "yh", "c"), None)
VMEM_LIMIT = 56 << 20


def dot(a, b, ca, cb):
    return lax.dot_general(a, b, (((ca,), (cb,)), ((), ())), preferred_element_type=F32)


def head_columns(h):
    return slice(h * DH, (h + 1) * DH), slice(HALF + h * DH, HALF + (h + 1) * DH)


def forward_kernel(qg_ref, kv_ref, out_ref, stats_ref, vt_ref):
    @pl.when(pl.program_id(0) == 0)
    def _():
        vt_ref[...] = kv_ref[:, HALF:].T

    logs, deltas = [], []
    for h in range(2):
        a, b = head_columns(h)
        scores = dot(kv_ref[:, a], qg_ref[:, a], 1, 1)
        top = jnp.max(scores, axis=0, keepdims=True)
        weights = jnp.exp2((scores - top) * SCALING2)
        total = jnp.sum(weights, axis=0, keepdims=True)
        out_t = dot(vt_ref[a, :], weights.astype(BF16), 1, 0) * (1.0 / total)
        out_ref[:, a] = out_t.T.astype(BF16)
        logs.append(top * SCALING2 + jnp.log2(total))
        deltas.append(jnp.sum(qg_ref[:, b].T.astype(F32) * out_t, axis=0, keepdims=True))
    stats_ref[...] = jnp.concatenate(logs + deltas, 0)


def forward(qg, kv, block):
    nq, nk = qg.shape[0], kv.shape[0]
    return pl.pallas_call(
        forward_kernel,
        grid=(nq // block,),
        in_specs=[
            pl.BlockSpec((block, 2 * HALF), lambda i: (i, 0)),
            pl.BlockSpec((nk, 2 * HALF), lambda i: (0, 0)),
        ],
        out_specs=[
            pl.BlockSpec((block, HALF), lambda i: (i, 0)),
            pl.BlockSpec((4, block), lambda i: (0, i)),
        ],
        out_shape=[
            jax.ShapeDtypeStruct((nq, HALF), BF16),
            jax.ShapeDtypeStruct((4, nq), F32),
        ],
        scratch_shapes=[pltpu.VMEM((HALF, nk), BF16)],
        compiler_params=pltpu.CompilerParams(vmem_limit_bytes=VMEM_LIMIT),
        name="forward",
    )(qg, kv)


def backward_kernel(steps, qg_ref, kv_ref, stats_ref, dq_ref, dkv_ref, kt_ref, sum_ref):
    i = pl.program_id(0)

    @pl.when(i == 0)
    def _():
        kt_ref[...] = kv_ref[:, :HALF].T

    for h in range(2):
        a, b = head_columns(h)
        log_total = stats_ref[h : h + 1, :]
        delta = stats_ref[2 + h : 3 + h, :]
        scores = dot(kv_ref[:, a], qg_ref[:, a], 1, 1)
        weights = jnp.exp2(scores * SCALING2 - log_total)
        upstream_dot = dot(kv_ref[:, b], qg_ref[:, b], 1, 1)
        score_grad = (weights * (upstream_dot - delta)).astype(BF16)
        dv = dot(weights.astype(BF16), qg_ref[:, b], 1, 0)
        dk = dot(score_grad, qg_ref[:, a], 1, 0) * SCALING
        dq_ref[:, a] = (dot(kt_ref[a, :], score_grad, 1, 0) * SCALING).T.astype(BF16)

        @pl.when(i == 0)
        def _():
            sum_ref[:, a] = dk
            sum_ref[:, b] = dv

        @pl.when(i > 0)
        def _():
            sum_ref[:, a] += dk
            sum_ref[:, b] += dv

    @pl.when(i == steps - 1)
    def _():
        dkv_ref[...] = sum_ref[...].astype(BF16)


def backward(qg, kv, stats, block):
    nq, nk = qg.shape[0], kv.shape[0]
    return pl.pallas_call(
        functools.partial(backward_kernel, nq // block),
        grid=(nq // block,),
        in_specs=[
            pl.BlockSpec((block, 2 * HALF), lambda i: (i, 0)),
            pl.BlockSpec((nk, 2 * HALF), lambda i: (0, 0)),
            pl.BlockSpec((4, block), lambda i: (0, i)),
        ],
        out_specs=[
            pl.BlockSpec((block, HALF), lambda i: (i, 0)),
            pl.BlockSpec((nk, 2 * HALF), lambda i: (0, 0)),
        ],
        out_shape=[
            jax.ShapeDtypeStruct((nq, HALF), BF16),
            jax.ShapeDtypeStruct((nk, 2 * HALF), BF16),
        ],
        scratch_shapes=[pltpu.VMEM((HALF, nk), BF16), pltpu.VMEM((nk, 2 * HALF), F32)],
        compiler_params=pltpu.CompilerParams(vmem_limit_bytes=VMEM_LIMIT),
        name="backward",
    )(qg, kv, stats)


def to_other_core(x):
    return lax.ppermute(x, "c", [(0, 1), (1, 0)])


def everyone(x, axes):
    peers = lax.axis_size(axes)
    return lax.all_to_all(
        jnp.broadcast_to(x[None], (peers,) + x.shape), axes, split_axis=0, concat_axis=0, tiled=True
    )


def owners_sum(x, axes):
    peers = lax.axis_size(axes)
    terms = lax.all_to_all(
        x.reshape(peers, x.shape[0] // peers, x.shape[1]), axes, split_axis=0, concat_axis=0, tiled=True
    )
    return jnp.sum(terms.astype(F32), axis=0)


def shards(queries, keys, values, upstream):
    core = lax.axis_index("c")
    rows = queries.shape[0]

    def halves(x):
        mine = jnp.where(core == 0, x[:, :HALF], x[:, HALF:])
        theirs = jnp.where(core == 0, x[:, HALF:], x[:, :HALF])
        return mine, theirs

    parts = [halves(x) for x in (queries, upstream, keys, values)]
    mine = jnp.concatenate([p[0] for p in parts], 1)
    theirs = to_other_core(jnp.concatenate([p[1] for p in parts], 1))
    both = jnp.concatenate([mine, theirs], 0)
    qg = everyone(both[:, : 2 * HALF], LINE).reshape(-1, 2 * HALF)
    kv = everyone(both[:, 2 * HALF :], PLANE).reshape(-1, 2 * HALF)

    out_part, stats_part = forward(qg, kv, 512)
    stats_all = everyone(stats_part, LINE)
    logs = stats_all[:, :2]
    top = jnp.max(logs, axis=0)
    log_total = top + jnp.log2(jnp.sum(jnp.exp2(logs - top), axis=0))
    delta = jnp.sum(jnp.exp2(logs - log_total) * stats_all[:, 2:], axis=0)
    stats = jnp.concatenate([log_total, delta], 0)
    own_scale = jnp.exp2(stats_part[:2] - log_total).T
    out_scaled = (out_part.reshape(-1, 2, DH) * own_scale[:, :, None]).astype(BF16).reshape(-1, HALF)

    dq_part, dkv_part = backward(qg, kv, stats, 512)
    attended = owners_sum(out_scaled, LINE)
    dq = owners_sum(dq_part, LINE)
    dkv = owners_sum(dkv_part, PLANE)
    results = jnp.concatenate([attended, dq, dkv], 1).astype(BF16)
    own, away = results[:rows], to_other_core(results[rows:])

    def whole(n):
        a, b = own[:, n * HALF : (n + 1) * HALF], away[:, n * HALF : (n + 1) * HALF]
        return jnp.concatenate([jnp.where(core == 0, a, b), jnp.where(core == 0, b, a)], 1)

    return whole(0), whole(1), whole(2), whole(3)


def solution(mesh):
    fine = Mesh(mesh.devices.reshape(2, 2, 4, 8, 2), ("yh", "c", "x", "z", "yl"))
    return jax.shard_map(
        shards, mesh=fine, in_specs=(TOKENS,) * 4, out_specs=(TOKENS,) * 4, check_vma=False
    )
```

```python
import functools
import math

import jax
import jax.numpy as jnp
from jax import lax
from jax.experimental import pallas as pl
from jax.experimental.pallas import tpu as pltpu
from jax.sharding import Mesh, PartitionSpec as P

DH = 128
HALF = 256
SCALING = 1.0 / math.sqrt(DH)
SCALING2 = SCALING * math.log2(math.e)
F32 = jnp.float32
BF16 = jnp.bfloat16
LINE = "z"
PLANE = ("yh", "x", "yl")
TOKENS = P(("x", "z", "yl", "yh", "c"), None)
VMEM_LIMIT = 56 << 20
BLOCK = 512
IN_VMEM = pl.BlockSpec(memory_space=pltpu.VMEM)
IN_SMEM = pl.BlockSpec(memory_space=pltpu.SMEM)


def dot(a, b, ca, cb):
    return lax.dot_general(a, b, (((ca,), (cb,)), ((), ())), preferred_element_type=F32)


def head_columns(h):
    return slice(h * DH, (h + 1) * DH), slice(HALF + h * DH, HALF + (h + 1) * DH)


def line_rows(z, step, size, rows):
    return pl.ds(pl.multiple_of(lax.rem(z + (step + size), size) * rows, rows), rows)


def forward_kernel(steps, z_ref, *refs):
    pieces, (kv_ref, out_ref, stats_ref, qg_ref, vt_ref) = refs[: len(steps)], refs[len(steps) :]
    rows = pieces[0].shape[0]
    for step, piece in zip(steps, pieces):
        qg_ref[line_rows(z_ref[0], step, len(steps), rows), :] = piece[...]
    vt_ref[...] = kv_ref[:, HALF:].T

    def block(i, carry):
        here = pl.ds(pl.multiple_of(i * BLOCK, BLOCK), BLOCK)
        logs, deltas = [], []
        for h in range(2):
            a, b = head_columns(h)
            scores = dot(kv_ref[:, a], qg_ref[here, a], 1, 1)
            top = jnp.max(scores, axis=0, keepdims=True)
            weights = jnp.exp2((scores - top) * SCALING2)
            total = jnp.sum(weights, axis=0, keepdims=True)
            out_t = dot(vt_ref[a, :], weights.astype(BF16), 1, 0) * (1.0 / total)
            out_ref[here, a] = out_t.T.astype(BF16)
            logs.append(top * SCALING2 + jnp.log2(total))
            deltas.append(jnp.sum(qg_ref[here, b].T.astype(F32) * out_t, axis=0, keepdims=True))
        stats = jnp.concatenate(logs + deltas, 0)
        for peer in range(stats_ref.shape[0]):
            stats_ref[peer, :, here] = stats
        return carry

    lax.fori_loop(0, qg_ref.shape[0] // BLOCK, block, 0)


def forward(z, steps, pieces, kv):
    nq, nk = pieces[0].shape[0] * len(steps), kv.shape[0]
    return pl.pallas_call(
        functools.partial(forward_kernel, steps),
        in_specs=[IN_SMEM] + [IN_VMEM] * (len(steps) + 1),
        out_specs=[IN_VMEM] * 3,
        out_shape=[
            jax.ShapeDtypeStruct((nq, HALF), BF16),
            jax.ShapeDtypeStruct((len(steps), 4, nq), F32),
            jax.ShapeDtypeStruct((nq, 2 * HALF), BF16),
        ],
        scratch_shapes=[pltpu.VMEM((HALF, nk), BF16)],
        compiler_params=pltpu.CompilerParams(vmem_limit_bytes=VMEM_LIMIT),
        name="forward",
    )(z, *pieces, kv)


def backward_kernel(steps, z_ref, qg_ref, kv_ref, stats_ref, *refs):
    dq_refs, (dkv_ref, dq_ref, kt_ref, sum_ref, merged_ref) = refs[: len(steps)], refs[len(steps) :]
    kt_ref[...] = kv_ref[:, :HALF].T
    logs = [stats_ref[j, 0:2, :] for j in range(len(steps))]
    top = functools.reduce(jnp.maximum, logs)
    log_total = top + jnp.log2(sum(jnp.exp2(x - top) for x in logs))
    merged_ref[0:2, :] = log_total
    merged_ref[2:4, :] = sum(
        jnp.exp2(x - log_total) * stats_ref[j, 2:4, :] for j, x in enumerate(logs)
    )
    sum_ref[...] = jnp.zeros_like(sum_ref)

    def block(i, carry):
        here = pl.ds(pl.multiple_of(i * BLOCK, BLOCK), BLOCK)
        for h in range(2):
            a, b = head_columns(h)
            log_total = merged_ref[h : h + 1, here]
            delta = merged_ref[2 + h : 3 + h, here]
            scores = dot(kv_ref[:, a], qg_ref[here, a], 1, 1)
            weights = jnp.exp2(scores * SCALING2 - log_total)
            upstream_dot = dot(kv_ref[:, b], qg_ref[here, b], 1, 1)
            score_grad = (weights * (upstream_dot - delta)).astype(BF16)
            sum_ref[:, b] += dot(weights.astype(BF16), qg_ref[here, b], 1, 0)
            sum_ref[:, a] += dot(score_grad, qg_ref[here, a], 1, 0) * SCALING
            dq_ref[here, a] = (dot(kt_ref[a, :], score_grad, 1, 0) * SCALING).T
        return carry

    lax.fori_loop(0, qg_ref.shape[0] // BLOCK, block, 0)
    dkv_ref[...] = sum_ref[...].astype(BF16)
    for step, ref in zip(steps, dq_refs):
        ref[...] = dq_ref[line_rows(z_ref[0], step, len(steps), ref.shape[0]), :]


def backward(z, steps, qg, kv, stats):
    nq, nk = qg.shape[0], kv.shape[0]
    out = pl.pallas_call(
        functools.partial(backward_kernel, steps),
        in_specs=[IN_SMEM] + [IN_VMEM] * 3,
        out_specs=[IN_VMEM] * (len(steps) + 1),
        out_shape=[jax.ShapeDtypeStruct((nq // len(steps), HALF), F32)] * len(steps)
        + [jax.ShapeDtypeStruct((nk, 2 * HALF), BF16)],
        scratch_shapes=[
            pltpu.VMEM((nq, HALF), F32),
            pltpu.VMEM((HALF, nk), BF16),
            pltpu.VMEM((nk, 2 * HALF), F32),
            pltpu.VMEM((4, nq), F32),
        ],
        compiler_params=pltpu.CompilerParams(vmem_limit_bytes=VMEM_LIMIT),
        name="backward",
    )(z, qg, kv, stats)
    return dict(zip(steps, out[:-1])), out[-1]


def to_other_core(x):
    return lax.ppermute(x, "c", [(0, 1), (1, 0)])


def along_line(x, by):
    size = lax.axis_size(LINE)
    return lax.ppermute(x, LINE, [(i, (i + by) % size) for i in range(size)])


def exchange(x, axes):
    return lax.all_to_all(x, axes, split_axis=0, concat_axis=0, tiled=True)


def shards(queries, keys, values, upstream):
    core = lax.axis_index("c")
    z = lax.axis_index(LINE).astype(jnp.int32).reshape(1)
    line = lax.axis_size(LINE)
    plane = lax.axis_size(PLANE)
    rows = queries.shape[0]

    def both_cores(*arrays):
        mine = [jnp.where(core == 0, x[:, :HALF], x[:, HALF:]) for x in arrays]
        theirs = [jnp.where(core == 0, x[:, HALF:], x[:, :HALF]) for x in arrays]
        away = to_other_core(jnp.concatenate(theirs, 1))
        return jnp.concatenate([jnp.concatenate(mine, 1), away], 0)

    kv = both_cores(keys, values)
    kv = exchange(jnp.broadcast_to(kv[None], (plane,) + kv.shape), PLANE).reshape(-1, 2 * HALF)
    pieces = {0: both_cores(queries, upstream)}
    for step in range(1, line // 2 + 1):
        pieces[-step] = along_line(pieces[1 - step], 1)
        if step < line // 2:
            pieces[step] = along_line(pieces[step - 1], -1)
    steps = sorted(pieces)

    out_part, stats_part, qg = forward(z, steps, [pieces[s] for s in steps], kv)
    stats = exchange(stats_part, LINE)
    out_parts = exchange(out_part.reshape(line, -1, HALF), LINE)

    dq_parts, dkv_part = backward(z, steps, qg, kv, stats)
    dkv_parts = exchange(dkv_part.reshape(plane, -1, 2 * HALF), PLANE)
    dq_up, dq_down = dq_parts[-line // 2], dq_parts[line // 2 - 1]
    dq_up = along_line(dq_up, -1)
    for step in range(line // 2 - 1, 0, -1):
        dq_up = along_line(dq_up + dq_parts[-step], -1)
        dq_down = along_line(dq_down, 1)
        if step > 1:
            dq_down = dq_down + dq_parts[step - 1]
    dq = dq_parts[0] + dq_up + dq_down

    own = lax.dynamic_slice_in_dim(stats[:, 0:2, :], z[0] * 2 * rows, 2 * rows, 2)
    top = jnp.max(own, axis=0)
    share = jnp.exp2(own - (top + jnp.log2(jnp.sum(jnp.exp2(own - top), axis=0))))
    share = jnp.repeat(share.transpose(0, 2, 1), DH, axis=2)
    attended = jnp.sum(out_parts.astype(F32) * share, axis=0)
    dkv = jnp.sum(dkv_parts.astype(F32), axis=0)
    results = jnp.concatenate([attended, dq, dkv], 1).astype(BF16)
    kept, away = results[:rows], to_other_core(results[rows:])

    def whole(n):
        a, b = kept[:, n * HALF : (n + 1) * HALF], away[:, n * HALF : (n + 1) * HALF]
        return jnp.concatenate([jnp.where(core == 0, a, b), jnp.where(core == 0, b, a)], 1)

    return whole(0), whole(1), whole(2), whole(3)


def solution(mesh):
    fine = Mesh(mesh.devices.reshape(2, 2, 4, 8, 2), ("yh", "c", "x", "z", "yl"))
    return jax.shard_map(
        shards, mesh=fine, in_specs=(TOKENS,) * 4, out_specs=(TOKENS,) * 4, check_vma=False
    )
```

```python
import functools
import math

import jax
import jax.numpy as jnp
from jax import lax
from jax.experimental import pallas as pl
from jax.experimental.pallas import tpu as pltpu
from jax.sharding import Mesh, PartitionSpec as P

DH = 128
PAIR = 2 * DH
SCALING = 1.0 / math.sqrt(DH)
SCALING2 = SCALING * math.log2(math.e)
F32 = jnp.float32
BF16 = jnp.bfloat16
LINE = "z"
PLANE = ("yh", "x", "yl")
TOKENS = P(("x", "z", "yl", "yh", "c"), None)
FORWARD_VMEM, BACKWARD_VMEM = 24 << 20, 32 << 20
IN_VMEM = pl.BlockSpec(memory_space=pltpu.VMEM)
IN_SMEM = pl.BlockSpec(memory_space=pltpu.SMEM)


def dot(a, b, ca, cb):
    return lax.dot_general(a, b, (((ca,), (cb,)), ((), ())), preferred_element_type=F32)


def in_line(z, step, size, width):
    return pl.ds(pl.multiple_of(lax.rem(z + (step + size), size) * width, width), width)


def rows_of(pieces, columns):
    return jnp.concatenate([p[:, columns] for p in pieces], 0)


FIRST, SECOND = slice(0, DH), slice(DH, PAIR)


def forward_kernel(count, *refs):
    pieces, refs = refs[: 2 * count], refs[2 * count :]
    kv_ref, outs, tops, stats_ref = refs[0], refs[1 : count + 1], refs[count + 1 : -1], refs[-1]
    values_t = kv_ref[:, SECOND].T
    for n in range(count):
        rows = pieces[2 * n : 2 * n + 2]
        scores = dot(kv_ref[:, FIRST], rows_of(rows, FIRST), 1, 1)
        top = jnp.max(scores, axis=0, keepdims=True)
        exp = jnp.exp2((scores - top) * SCALING2)
        total = jnp.sum(exp, axis=0, keepdims=True)
        out_t = dot(values_t, exp.astype(BF16), 1, 0)
        outs[n][...] = out_t
        tops[n][...] = top * SCALING2
        here = slice(n * out_t.shape[1], (n + 1) * out_t.shape[1])
        stats_ref[0:1, here] = top * SCALING2 + jnp.log2(total)
        stats_ref[1:2, here] = (
            jnp.sum(rows_of(rows, SECOND).T.astype(F32) * out_t, axis=0, keepdims=True) / total
        )


def forward(pieces, kv):
    count, width = len(pieces) // 2, 2 * pieces[0].shape[0]
    got = pl.pallas_call(
        functools.partial(forward_kernel, count),
        in_specs=[IN_VMEM] * (len(pieces) + 1),
        out_specs=[IN_VMEM] * (2 * count + 1),
        out_shape=[jax.ShapeDtypeStruct((n, width), F32) for n in (DH, 1) for _ in range(count)]
        + [jax.ShapeDtypeStruct((2, count * width), F32)],
        compiler_params=pltpu.CompilerParams(vmem_limit_bytes=FORWARD_VMEM),
        name="forward",
    )(*pieces, kv)
    return [got[n : 2 * count : count] for n in range(count)], got[-1]


def backward_kernel(steps, carried, last, size, z_ref, *refs):
    count = len(steps)
    pieces, refs = refs[:count], refs[count:]
    saved, refs = refs[:count], refs[count:]
    stats_ref, kv_ref, refs = refs[0], refs[1], refs[2:]
    if carried:
        start_ref, refs = refs[0], refs[1:]
    grads, dkv_ref, merged_ref = refs[:count], refs[count], refs[-1]
    sum_ref = refs[count + 1] if last else dkv_ref
    width = pieces[0].shape[0]
    z = z_ref[0]
    logs = [stats_ref[j, 0:1, :] for j in range(size)]
    top = functools.reduce(jnp.maximum, logs)
    log_total = top + jnp.log2(sum(jnp.exp2(x - top) for x in logs))
    merged_ref[0:1, :] = log_total
    merged_ref[1:2, :] = sum(jnp.exp2(x - log_total) * stats_ref[j, 1:2, :] for j, x in enumerate(logs))
    keys_t = kv_ref[:, FIRST].T
    for n in range(count // 2):
        rows = pieces[2 * n : 2 * n + 2]
        out_ref, top_ref = saved[2 * n : 2 * n + 2]
        where = [in_line(z, step, size, width) for step in steps[2 * n : 2 * n + 2]]
        log_total, delta = [jnp.concatenate([merged_ref[k : k + 1, w] for w in where], 1) for k in range(2)]
        share = jnp.exp2(top_ref[...] - log_total)
        scores = dot(kv_ref[:, FIRST], rows_of(rows, FIRST), 1, 1)
        weights = jnp.exp2(scores * SCALING2 - log_total)
        upstream_dot = dot(kv_ref[:, SECOND], rows_of(rows, SECOND), 1, 1)
        score_grad = (weights * (upstream_dot - delta)).astype(BF16)
        dv = dot(weights.astype(BF16), rows_of(rows, SECOND), 1, 0)
        dk = dot(score_grad, rows_of(rows, FIRST), 1, 0) * SCALING
        if n == 0 and not carried:
            sum_ref[:, FIRST] = dk
            sum_ref[:, SECOND] = dv
        else:
            before = start_ref if n == 0 else sum_ref
            sum_ref[:, FIRST] = before[:, FIRST] + dk
            sum_ref[:, SECOND] = before[:, SECOND] + dv
        dq_t = dot(keys_t, score_grad, 1, 0) * SCALING
        out_t = out_ref[...] * share
        for k in range(2):
            here = slice(k * width, (k + 1) * width)
            grads[2 * n + k][:, FIRST] = out_t[:, here].T.astype(BF16)
            grads[2 * n + k][:, SECOND] = dq_t[:, here].T.astype(BF16)
    if last:
        high = sum_ref[...].astype(BF16)
        dkv_ref[:, :PAIR] = high
        dkv_ref[:, PAIR:] = (sum_ref[:, FIRST] - high[:, FIRST].astype(F32)).astype(BF16)


def backward(z, steps, pieces, saved, stats, kv, carried, last):
    size, _, nq = stats.shape
    nk, width = kv.shape[0], pieces[0].shape[0]
    got = pl.pallas_call(
        functools.partial(backward_kernel, steps, len(carried), last, size),
        in_specs=[IN_SMEM] + [IN_VMEM] * (len(pieces) + len(saved) + 2 + len(carried)),
        out_specs=[IN_VMEM] * (len(steps) + 1),
        out_shape=[jax.ShapeDtypeStruct((width, PAIR), BF16)] * len(steps)
        + [jax.ShapeDtypeStruct((nk, 3 * DH), BF16) if last else jax.ShapeDtypeStruct((nk, PAIR), F32)],
        scratch_shapes=[pltpu.VMEM((nk, PAIR), F32)] * last + [pltpu.VMEM((2, nq), F32)],
        compiler_params=pltpu.CompilerParams(vmem_limit_bytes=BACKWARD_VMEM),
        name="backward",
    )(z, *pieces, *saved, stats, kv, *carried)
    return dict(zip(steps, got[:-1])), got[-1]


def join_kernel(core_ref, kept_ref, away_ref, *out_refs):
    first = core_ref[0] == 0
    for n, ref in enumerate(out_refs):
        here = slice(n * PAIR, (n + 1) * PAIR)
        a, b = kept_ref[:, here], away_ref[:, here]
        ref[:, :PAIR] = jnp.where(first, a, b)
        ref[:, PAIR:] = jnp.where(first, b, a)


def join_heads(core, kept, away):
    shape = jax.ShapeDtypeStruct((kept.shape[0], 2 * PAIR), BF16)
    return pl.pallas_call(
        join_kernel,
        in_specs=[IN_SMEM] + [IN_VMEM] * 2,
        out_specs=[IN_VMEM] * 4,
        out_shape=[shape] * 4,
        compiler_params=pltpu.CompilerParams(vmem_limit_bytes=4 << 20),
        name="join_heads",
    )(core, kept, away)


def swapped(x, axis):
    return lax.ppermute(x, axis, [(0, 1), (1, 0)])


def along_line(x, by):
    size = lax.axis_size(LINE)
    return lax.ppermute(x, LINE, [(i, (i + by) % size) for i in range(size)])


def along_line_and_across(x, by):
    size = lax.axis_size(LINE)
    pairs = [(2 * i + j, 2 * ((i + by) % size) + 1 - j) for i in range(size) for j in range(2)]
    return lax.ppermute(x, (LINE, "yl"), pairs)


def exchange(x, axes):
    return lax.all_to_all(x, axes, split_axis=0, concat_axis=0, tiled=True)


def add(a, b):
    return (a.astype(F32) + b.astype(F32)).astype(BF16)


def split(which, *arrays):
    halves = [(x[:, : x.shape[1] // 2], x[:, x.shape[1] // 2 :]) for x in arrays]
    kept = [jnp.where(which == 0, a, b) for a, b in halves]
    sent = [jnp.where(which == 0, b, a) for a, b in halves]
    return jnp.concatenate(kept, 1), jnp.concatenate(sent, 1)


def joined(which, mine, other):
    return jnp.concatenate([jnp.where(which == 0, mine, other), jnp.where(which == 0, other, mine)], 1)


def shards(queries, keys, values, upstream):
    core, low = lax.axis_index("c"), lax.axis_index("yl")
    core1 = core.astype(jnp.int32).reshape(1)
    z = lax.axis_index(LINE).astype(jnp.int32).reshape(1)
    line, plane = lax.axis_size(LINE), lax.axis_size(PLANE)
    rows = queries.shape[0]

    kept_kv, sent_kv = split(core, keys, values)
    kept, sent = split(core, queries, upstream)
    qg = jnp.concatenate([kept, swapped(sent, "c")], 0)
    kept, sent = split(low, qg[:, :PAIR], qg[:, PAIR:])
    pieces = {0: jnp.concatenate([kept, swapped(sent, "yl")], 0)}
    sent_kv, qg = lax.optimization_barrier((sent_kv, qg))
    kv = jnp.concatenate([kept_kv, swapped(sent_kv, "c")], 0)
    kv = jnp.stack([jnp.concatenate([kv[:, i : i + DH], kv[:, PAIR + i : PAIR + i + DH]], 1) for i in (0, DH)])
    kv = jnp.broadcast_to(kv[None], (plane // 2,) + kv.shape).reshape((plane,) + kv.shape[1:])
    kv = exchange(kv, PLANE).reshape(-1, PAIR)

    for step in range(1, line // 2 + 1):
        pieces[-step] = along_line(pieces[1 - step], 1)
        if step < line // 2:
            pieces[step] = along_line(pieces[step - 1], -1)
    groups = [[0, -1, 1, -2], [2, -3], [3, -4]]
    steps = sum(groups, [])
    parts = [forward([pieces[s] for s in group], kv) for group in groups]
    stats = jnp.concatenate([p[1] for p in parts], 1).reshape(2, line, 4 * rows)
    saved = dict(zip(steps[::2], sum([p[0] for p in parts], [])))
    source = jnp.argsort(jnp.array(steps) % line)
    stats = jnp.take(stats, source[(jnp.arange(line) - z) % line], axis=1).reshape(1, 2, -1)
    stats = exchange(jnp.broadcast_to(stats, (line,) + stats.shape[1:]), LINE)

    def backward_of(group, carried, last):
        kept = [x for s in group[::2] for x in saved[s]]
        return backward(z, group, [pieces[s] for s in group], kept, stats, kv, carried, last)

    grads, dkv_part = backward_of([3, -4], (), False)
    up, down = along_line(grads[-4], -1), along_line(grads[3], 1)
    more, dkv_part = backward_of([2, -3, 1, -2], (dkv_part,), False)
    grads.update(more)
    dkv_part, up, down = lax.optimization_barrier((dkv_part, up, down))
    up, down = along_line(add(up, grads[-3]), -1), along_line(add(down, grads[2]), 1)
    more, dkv_part = backward_of([0, -1], (dkv_part,), True)
    grads.update(more)
    dkv_parts = exchange(dkv_part.reshape(plane, -1, 3 * DH), PLANE)
    up, down = along_line(add(up, grads[-2]), -1), along_line(add(down, grads[1]), 1)
    near = 2 * rows
    up = add(up, grads[-1])
    own = add(down, grads[0])
    mine = add(along_line(up[:near], -1), own[:near])
    other = add(along_line_and_across(up[near:], -1), swapped(own[near:], "yl"))
    dkv = jnp.sum(dkv_parts.astype(F32).reshape(plane // 2, 2, 2 * rows, 3 * DH), axis=0)
    dkv = jnp.concatenate([dkv[:, :, :DH] + dkv[:, :, PAIR:], dkv[:, :, DH:PAIR]], 2).astype(BF16)
    results = jnp.concatenate(
        [joined(low, mine[:, FIRST], other[:, FIRST]), joined(low, mine[:, SECOND], other[:, SECOND])]
        + [dkv[i, :, columns] for columns in (FIRST, SECOND) for i in (0, 1)],
        1,
    )
    kept, away = results[:rows], swapped(results[rows:], "c")
    return tuple(join_heads(core1, kept, away))


def solution(mesh):
    fine = Mesh(mesh.devices.reshape(2, 2, 4, 8, 2), ("yh", "c", "x", "z", "yl"))
    return jax.shard_map(
        shards, mesh=fine, in_specs=(TOKENS,) * 4, out_specs=(TOKENS,) * 4, check_vma=False
    )
```
